32 devices in a mesh: fsdp: 8 (over z, y), dp: 4 (over x, core).
Axes of the slice: x: 2, y: 2, z: 4, core: 2. Of those that a mesh axis runs over, the one named last changes fastest.
Arguments:
- tokens: bfloat16 [4096, 4096], P(('fsdp', 'dp')), may hold values from -6 to 6
- gain: float32 [4096], replicated, may hold values from 0.5 to 1.5
- tiles: bfloat16 [128, 128, 128], P('fsdp'), may hold values from -0.5 to 0.5
- tile_rows: int32 [128], replicated, may hold values from 0 to 31, as said below
- tile_cols: int32 [128], replicated, may hold values from 0 to 111, as said below
- cotangent: bfloat16 [4096, 14336], P(('fsdp', 'dp')), may hold values from -6 to 6
Outputs:
- projected: bfloat16 [4096, 14336], P(('fsdp', 'dp'))
- token_grad: bfloat16 [4096, 4096], P(('fsdp', 'dp'))
- tile_grad: float32 [128, 128, 128], P('fsdp')
- gain_grad: float32 [4096], replicated
The draws below stay inside these ranges and needn't reach their ends.
Inputs may be any that keep to these rules, and one draw needn't show every extreme that they name: The pairs (tile_rows[i], tile_cols[i]) are all different. `tile_cols`: pairs with tile_rows as above.
All inputs are finite; a program needn't handle non-finite values.
Results may differ from the reference program's by a relative error of at most 0.0049.
Values may be sent and summed in bfloat16 or wider, within the bound.
A program may use at most 256 MiB of HBM per device.

```python
import jax
import jax.numpy as jnp
from jax import lax

D = 4096
FF = 14336
TILE = 128
NNZ = 128
RB = 32
CB = 112
TOKENS = 4096
N_FSDP = 8


def tile_places(key):
    inner = jax.random.fold_in(key, 7)
    total = RB * CB
    rest = 1 + jax.random.permutation(inner, total - 2)[:NNZ - 2]
    first = jnp.array([total - 1, 0], dtype=jnp.int32)
    return jnp.concatenate([first, rest.astype(jnp.int32)])


def draw_tile_rows(key, part):
    return (tile_places(key) // CB).astype(jnp.int32)


def draw_tile_cols(key, part):
    return (tile_places(key) % CB).astype(jnp.int32)


def levels(stream_key, extent, shards, low, top_value):
    loudness, own = 1.0, jax.random.fold_in(stream_key, 6)
    for axis_at, shards_of in shards:
        steps = jnp.exp(jax.random.uniform(jax.random.fold_in(own, axis_at), (shards_of,), jnp.float32, low / len(shards), top_value / len(shards)))
        loudness = loudness * jnp.repeat(steps, extent[axis_at] // shards_of).reshape([-1 if axis == axis_at else 1 for axis in range(len(extent))])
    return loudness


def normal_values(key, shape, width, bound, cuts=(), held_as=jnp.bfloat16):
    drawn = jax.random.normal(key, shape, jnp.float32) * width
    if len(cuts) > 0:
        drawn = levels(key, shape, cuts, -0.22, 0.18) * drawn
    return jnp.clip(drawn, min=-bound, max=bound).astype(held_as)


def setup_inputs(seed: int = 0) -> dict:
    key_list = jax.random.split(jax.random.key(seed), 7)
    tokens = normal_values(key_list[0], (TOKENS, D), 1.0, 6.0, ((0, 32),))
    gain = jnp.clip(jax.random.uniform(key_list[1], (D,), jnp.float32, 0.5, 1.5), 0.5, 1.5)
    tiles = normal_values(key_list[2], (NNZ, TILE, TILE), (TILE * NNZ // CB) ** -0.5, 0.5, ((0, 8),))
    tile_rows = draw_tile_rows(jax.random.fold_in(key_list[6], 71), 0)
    tile_cols = draw_tile_cols(jax.random.fold_in(key_list[6], 71), 0)
    cotangent = normal_values(key_list[5], (TOKENS, FF), 1.0, 6.0, ((0, 32),))
    return dict(tokens=tokens, gain=gain, tiles=tiles, tile_rows=tile_rows, tile_cols=tile_cols, cotangent=cotangent)


def reference(tokens, gain, tiles, tile_rows, tile_cols, cotangent):
    x32 = tokens.astype(jnp.float32)
    scale = lax.rsqrt(lax.optimization_barrier(jnp.mean(x32 * x32, axis=-1, keepdims=True)) + 1e-05)
    normed = (x32 * scale * gain).astype(jnp.bfloat16)
    xblocks = normed.reshape(TOKENS, RB, TILE)
    gblocks = cotangent.reshape(TOKENS, CB, TILE)
    block = TOKENS // N_FSDP

    def one_block(index):
        xpart = lax.dynamic_slice_in_dim(xblocks, index * block, block, 0)
        gpart = lax.dynamic_slice_in_dim(gblocks, index * block, block, 0)

        def step(carry, which):
            outsum, back = carry
            row_id = tile_rows[which]
            col_id = tile_cols[which]
            weight = tiles[which]
            xrow = lax.dynamic_index_in_dim(xpart, row_id, 1, keepdims=False)
            gcol = lax.dynamic_index_in_dim(gpart, col_id, 1, keepdims=False)
            outsum = outsum.at[:, col_id].add(jnp.dot(xrow, weight, preferred_element_type=jnp.float32))
            back = back.at[:, row_id].add(jnp.dot(gcol, weight.T, preferred_element_type=jnp.float32))
            return ((outsum, back), None)
        start = (jnp.zeros((block, CB, TILE), jnp.float32), jnp.zeros((block, RB, TILE), jnp.float32))
        (outsum, back), _ = lax.scan(step, start, jnp.arange(NNZ, dtype=jnp.int32))
        return (outsum, back)
    outsum, back = lax.map(one_block, jnp.arange(N_FSDP, dtype=jnp.int32))
    projected = outsum.reshape(TOKENS, FF).astype(jnp.bfloat16)
    dnormed = back.reshape(TOKENS, D)
    gain_grad = lax.optimization_barrier(jnp.sum(dnormed * x32 * scale, axis=0))
    inner = lax.optimization_barrier(jnp.mean(x32 * gain * dnormed, axis=-1, keepdims=True))
    token_grad = (scale * gain * dnormed - x32 * scale ** 3 * inner).astype(jnp.bfloat16)

    def tile_term(which):
        xrow = lax.dynamic_index_in_dim(xblocks, tile_rows[which], 1, keepdims=False)
        gcol = lax.dynamic_index_in_dim(gblocks, tile_cols[which], 1, keepdims=False)
        return jnp.dot(xrow.T, gcol, preferred_element_type=jnp.float32)
    tile_grad = lax.map(tile_term, jnp.arange(NNZ, dtype=jnp.int32))
    return (projected, token_grad, tile_grad, gain_grad)
```

```python
import functools

import jax
import jax.numpy as jnp
from jax import lax
from jax.experimental import pallas as pl
from jax.experimental.pallas import tpu as pltpu
from jax.sharding import PartitionSpec as P

MESH = pl.DeviceIdType.MESH
F32 = jnp.float32
BF16 = jnp.bfloat16
UNROLL = 8


def remote(src, dst, send, recv, f, d):
    return pltpu.make_async_remote_copy(
        src_ref=src, dst_ref=dst, send_sem=send, recv_sem=recv,
        device_id={"fsdp": f, "dp": d}, device_id_type=MESH,
    )


def row_scale(tok_ref, width, tile):
    total = jnp.zeros((tok_ref.shape[0], tile), F32)
    for b in range(width // tile):
        x = tok_ref[:, b * tile:(b + 1) * tile].astype(F32)
        total = total + x * x
    mean = jnp.sum(total, axis=-1, keepdims=True) / width
    return lax.rsqrt(mean + 1e-05)


def grads_kernel(rows_ref, cols_ref, tok_ref, gain_ref, cot_ref, part_ref, normed_t):
    number, tile = part_ref.shape[0], part_ref.shape[1]
    width = tok_ref.shape[1]
    scale = row_scale(tok_ref, width, tile)
    for b in range(width // tile):
        at = slice(b * tile, (b + 1) * tile)
        x = tok_ref[:, at].astype(F32)
        normed_t[b] = (x * scale * gain_ref[:, at]).T.astype(BF16)

    def body(i, carry):
        terms = []
        for u in range(UNROLL):
            k = i * UNROLL + u
            col = pl.multiple_of(cols_ref[k] * tile, tile)
            terms.append(jnp.dot(normed_t[rows_ref[k]], cot_ref[:, pl.ds(col, tile)], preferred_element_type=F32))
        for u in range(UNROLL):
            part_ref[i * UNROLL + u] = terms[u].astype(BF16)
        return carry

    lax.fori_loop(0, number // UNROLL, body, 0)


def comm_kernel(
    A, tiles_ref, part_ref, ag, out_ref,
    rc, ry, rz, xs, rx,
    lsem, cs, cr, ys, yr, zs, zr, xss, xrs, fs, fr,
    ays, ayr, azs, azr, axs, axr, acs, acr,
):
    f, d = lax.axis_index("fsdp"), lax.axis_index("dp")
    z, y = f // 2, f % 2
    x, c = d // 2, d % 2
    fy = z * 2 + (1 - y)
    dc = x * 2 + (1 - c)
    dx = (1 - x) * 2 + c
    dxc = (1 - x) * 2 + (1 - c)
    group = tiles_ref.shape[0]
    h, q = group // 2, group // 4
    has_left, has_right = z > 0, z < A - 1

    barrier = pltpu.get_barrier_semaphore()

    def greet(ff, dd):
        pl.semaphore_signal(barrier, inc=1, device_id={"fsdp": ff, "dp": dd}, device_id_type=MESH)

    greet(f, dc)
    greet(f, dx)
    greet(fy, d)
    pl.when(has_left)(lambda: greet(f - 2, d))
    pl.when(has_right)(lambda: greet(f + 2, d))
    pl.semaphore_wait(barrier, 3 + has_left.astype(jnp.int32) + has_right.astype(jnp.int32))

    def quarter(fb, dd):
        return ag.at[fb, pl.ds(dd * q, q)]

    def to_core(b, yy):
        fb = b * 2 + yy
        return remote(part_ref.at[fb, pl.ds((1 - c) * h, h)], rc.at[fb], cs.at[fb], cr.at[fb], f, dc)

    def to_y(b):
        return remote(rc.at[b * 2 + 1 - y], ry.at[b], ys.at[b], yr.at[b], fy, d)

    def to_right(b):
        return remote(rc.at[b * 2 + y], rz.at[b], zs.at[b], zr.at[b], f + 2, d)

    def to_left(b):
        slot = jnp.where(b == z - 1, A, b)
        return remote(rc.at[b * 2 + y], rz.at[slot], zs.at[b], zr.at[slot], f - 2, d)

    def arrived(slot):
        remote(rz.at[slot], rz.at[slot], zs.at[0], zr.at[slot], fy, d).wait_recv()

    own = tiles_ref.at[pl.ds(d * q, q)]
    own_y = remote(own, quarter(f, d), ays, ayr, fy, d)

    def ag_left(fb, src):
        return remote(src, quarter(fb, d), azs.at[0, fb], azr.at[fb], f - 2, d)

    def ag_right(fb, src):
        return remote(src, quarter(fb, d), azs.at[1, fb], azr.at[fb], f + 2, d)

    def ag_x(fb):
        return remote(quarter(fb, d), quarter(fb, d), axs.at[fb], axr.at[fb], f, dx)

    def ag_core(fb, which):
        dd = d if which == 0 else dx
        return remote(quarter(fb, dd), quarter(fb, dd), acs.at[which, fb], acr.at[which, fb], f, dc)

    def ag_landed(fb, dd, sem):
        remote(quarter(fb, dd), quarter(fb, dd), ays, sem, fy, d).wait_recv()

    def spread(fb):
        ag_x(fb).start()
        ag_core(fb, 0).start()

    own_y.start()
    pl.when(has_left)(lambda: ag_left(f, own).start())
    pl.when(has_right)(lambda: ag_right(f, own).start())
    for b in range(A):
        to_core(b, 1 - y).start()
    for b in range(A):
        to_core(b, y).start()
    keep = pltpu.make_async_copy(tiles_ref, ag.at[f], lsem)
    keep.start()

    def halves(fb):
        return part_ref[fb, pl.ds(c * h, h)].astype(F32) + rc[fb].astype(F32)

    for b in range(A):
        fb = b * 2 + 1 - y
        to_core(b, 1 - y).wait_recv()
        rc[fb] = halves(fb).astype(BF16)
        to_y(b).start()

    ag_landed(fy, d, ayr)
    pl.when(has_left)(lambda: ag_left(fy, quarter(fy, d)).start())
    pl.when(has_right)(lambda: ag_right(fy, quarter(fy, d)).start())
    spread(fy)

    def summed(b):
        to_core(b, y).wait_recv()
        to_y(b).wait_recv()
        return halves(b * 2 + y) + ry[b].astype(F32)

    def gather_from_left(s):
        b = z - s
        for yy in range(2):
            fb = b * 2 + yy
            ag_landed(fb, d, azr.at[fb])
            pl.when(has_right)(lambda: ag_right(fb, quarter(fb, d)).start())
            spread(fb)

    def gather_from_right(s):
        b = z + s
        for yy in range(2):
            fb = b * 2 + yy
            ag_landed(fb, d, azr.at[fb])
            pl.when(has_left)(lambda: ag_left(fb, quarter(fb, d)).start())
            spread(fb)

    def send_sum_right(s):
        b = z + s
        fb = b * 2 + y
        rc[fb] = summed(b).astype(BF16)

        @pl.when(has_left)
        def _():
            arrived(b)
            rc[fb] = (rc[fb].astype(F32) + rz[b].astype(F32)).astype(BF16)

        to_right(b).start()

    def send_sum_left(s):
        b = z - s
        fb = b * 2 + y
        rc[fb] = summed(b).astype(BF16)

        @pl.when(has_right)
        def _():
            arrived(b)
            rc[fb] = (rc[fb].astype(F32) + rz[b].astype(F32)).astype(BF16)

        to_left(b).start()

    for s in range(1, A):
        far = A - s
        pl.when(z + far < A)(functools.partial(send_sum_right, far))
        pl.when(z - far >= 0)(functools.partial(send_sum_left, far))
        pl.when(z - s >= 0)(functools.partial(gather_from_left, s))
        pl.when(z + s < A)(functools.partial(gather_from_right, s))

    mine = pl.ds(c * h, h)
    out_ref[mine] = summed(z)

    @pl.when(has_left)
    def _():
        arrived(z)
        out_ref[mine] = out_ref[mine] + rz[z].astype(F32)

    @pl.when(has_right)
    def _():
        arrived(A)
        out_ref[mine] = out_ref[mine] + rz[A].astype(F32)

    xs[...] = out_ref[mine].astype(BF16)
    across = remote(xs, rx, xss, xrs, f, dx)
    across.start()

    def visit(fn):
        fn(fy)
        for s in range(1, A):
            @pl.when(z - s >= 0)
            def _():
                fn((z - s) * 2)
                fn((z - s) * 2 + 1)

            @pl.when(z + s < A)
            def _():
                fn((z + s) * 2)
                fn((z + s) * 2 + 1)

    def relay(fb):
        ag_landed(fb, dx, axr.at[fb])
        ag_core(fb, 1).start()

    visit(relay)

    across.wait_recv()
    out_ref[mine] = xs[...].astype(F32) + rx[...].astype(F32)
    last = remote(out_ref.at[mine], out_ref.at[mine], fs, fr, f, dc)
    last.start()

    def finish(fb):
        ag_landed(fb, dc, acr.at[0, fb])
        ag_landed(fb, dxc, acr.at[1, fb])
        ag_x(fb).wait_send()
        ag_core(fb, 0).wait_send()
        ag_core(fb, 1).wait_send()

    visit(finish)

    other = out_ref.at[pl.ds((1 - c) * h, h)]
    remote(other, other, fs, fr, f, dc).wait_recv()
    last.wait_send()
    across.wait_send()
    keep.wait()
    own_y.wait_send()
    for fb in (f, fy):
        pl.when(has_left)(lambda: ag_left(fb, own).wait_send())
        pl.when(has_right)(lambda: ag_right(fb, own).wait_send())
    for b in range(A):
        to_core(b, 0).wait_send()
        to_core(b, 1).wait_send()
        to_y(b).wait_send()
    for s in range(1, A):
        @pl.when(z + s < A)
        def _():
            to_right(z + s).wait_send()
            for yy in range(2):
                pl.when(has_left)(lambda: ag_left((z + s) * 2 + yy, own).wait_send())

        @pl.when(z - s >= 0)
        def _():
            to_left(z - s).wait_send()
            for yy in range(2):
                pl.when(has_right)(lambda: ag_right((z - s) * 2 + yy, own).wait_send())


def apply_kernel(
    rows_ref, cols_ref, tok_ref, gain_ref, tiles_ref, cot_ref, proj_ref, tgrad_ref, ggrad_ref,
    normed, outsum, back,
):
    number, tile = tiles_ref.shape[0], tiles_ref.shape[1]
    count, width = tok_ref.shape
    scale = row_scale(tok_ref, width, tile)
    for b in range(width // tile):
        at = slice(b * tile, (b + 1) * tile)
        normed[b] = (tok_ref[:, at].astype(F32) * scale * gain_ref[:, at]).astype(BF16)
        back[b] = jnp.zeros((count, tile), F32)

    def clear(b, carry):
        outsum[b] = jnp.zeros((count, tile), F32)
        return carry

    lax.fori_loop(0, outsum.shape[0], clear, 0)

    def body(i, carry):
        forward, backward, places = [], [], []
        for u in range(UNROLL):
            k = i * UNROLL + u
            r, c = rows_ref[k], cols_ref[k]
            places.append((r, c))
            weight = tiles_ref[k]
            g = cot_ref[:, pl.ds(pl.multiple_of(c * tile, tile), tile)]
            forward.append(jnp.dot(normed[r], weight, preferred_element_type=F32))
            backward.append(lax.dot_general(g, weight, (((1,), (1,)), ((), ())), preferred_element_type=F32))
        for u in range(UNROLL):
            r, c = places[u]
            outsum[c] = outsum[c] + forward[u]
            back[r] = back[r] + backward[u]
        return carry

    lax.fori_loop(0, number // UNROLL, body, 0)

    inner = jnp.zeros((count, tile), F32)
    for b in range(width // tile):
        at = slice(b * tile, (b + 1) * tile)
        x = tok_ref[:, at].astype(F32)
        dn = back[b]
        inner = inner + x * gain_ref[:, at] * dn
        ggrad_ref[b:b + 1, :] = jnp.sum(dn * x * scale, axis=0, keepdims=True)
    inner = jnp.sum(inner, axis=-1, keepdims=True) / width
    weight = scale * scale * scale * inner
    for b in range(width // tile):
        at = slice(b * tile, (b + 1) * tile)
        x = tok_ref[:, at].astype(F32)
        tgrad_ref[:, at] = (scale * gain_ref[:, at] * back[b] - x * weight).astype(BF16)
    for b in range(outsum.shape[0]):
        proj_ref[:, b * tile:(b + 1) * tile] = outsum[b].astype(BF16)


def gain_kernel(steps, part_ref, out_ref, acc, got, ssem, rsem):
    f, d = lax.axis_index("fsdp"), lax.axis_index("dp")

    def partner(step):
        axis, bit = step
        me = f if axis == "fsdp" else d
        there = me + bit - 2 * bit * ((me // bit) % 2)
        return (there, d) if axis == "fsdp" else (f, there)

    barrier = pltpu.get_barrier_semaphore()
    for step in steps:
        ff, dd = partner(step)
        pl.semaphore_signal(barrier, inc=1, device_id={"fsdp": ff, "dp": dd}, device_id_type=MESH)
    pl.semaphore_wait(barrier, len(steps))
    acc[0] = part_ref[...]
    for i, step in enumerate(steps):
        ff, dd = partner(step)
        copy = remote(acc.at[i], got.at[i], ssem.at[i], rsem.at[i], ff, dd)
        copy.start()
        copy.wait()
        acc[i + 1] = acc[i] + got[i]
    out_ref[...] = acc[len(steps)]


def bits(axis, size):
    found, bit = [], 1
    while bit < size:
        found.append((axis, bit))
        bit *= 2
    return found


def solution(mesh):
    nf, nd = mesh.shape["fsdp"], mesh.shape["dp"]
    A = nf // 2
    steps = bits("dp", nd) + bits("fsdp", nf)
    vmem = pl.BlockSpec(memory_space=pltpu.VMEM)
    smem = pl.BlockSpec(memory_space=pltpu.SMEM)
    anywhere = pl.BlockSpec(memory_space=pl.ANY)
    dma = pltpu.SemaphoreType.DMA
    params = functools.partial(pltpu.CompilerParams, vmem_limit_bytes=60 * 2**20)

    def shards(tokens, gain, tiles, tile_rows, tile_cols, cotangent):
        count, width = tokens.shape
        group, tile, _ = tiles.shape
        number = group * nf
        rb, cb = width // tile, cotangent.shape[1] // tile
        h = group // 2
        gain2 = gain.reshape(1, width)

        part = pl.pallas_call(
            grads_kernel,
            out_shape=jax.ShapeDtypeStruct((number, tile, tile), BF16),
            in_specs=[smem, smem, vmem, vmem, vmem],
            out_specs=vmem,
            scratch_shapes=[pltpu.VMEM((rb, tile, count), BF16)],
            compiler_params=params(),
        )(tile_rows, tile_cols, tokens, gain2, cotangent)

        gathered, tile_grad = pl.pallas_call(
            functools.partial(comm_kernel, A),
            out_shape=(
                jax.ShapeDtypeStruct((nf, group, tile, tile), BF16),
                jax.ShapeDtypeStruct((group, tile, tile), F32),
            ),
            in_specs=[anywhere, vmem],
            out_specs=(anywhere, vmem),
            scratch_shapes=[
                pltpu.VMEM((nf, h, tile, tile), BF16),
                pltpu.VMEM((A, h, tile, tile), BF16),
                pltpu.VMEM((A + 1, h, tile, tile), BF16),
                pltpu.VMEM((h, tile, tile), BF16),
                pltpu.VMEM((h, tile, tile), BF16),
                dma,
                dma((nf,)), dma((nf,)),
                dma((A,)), dma((A,)),
                dma((A,)), dma((A + 1,)),
                dma, dma, dma, dma,
                dma, dma,
                dma((2, nf)), dma((nf,)),
                dma((nf,)), dma((nf,)),
                dma((2, nf)), dma((2, nf)),
            ],
            compiler_params=params(collective_id=0, has_side_effects=True),
        )(tiles, part.reshape(nf, group, tile, tile))

        projected, token_grad, gain_part = pl.pallas_call(
            apply_kernel,
            out_shape=(
                jax.ShapeDtypeStruct(cotangent.shape, BF16),
                jax.ShapeDtypeStruct(tokens.shape, BF16),
                jax.ShapeDtypeStruct((rb, tile), F32),
            ),
            in_specs=[smem, smem, vmem, vmem, vmem, vmem],
            out_specs=(vmem, vmem, vmem),
            scratch_shapes=[
                pltpu.VMEM((rb, count, tile), BF16),
                pltpu.VMEM((cb, count, tile), F32),
                pltpu.VMEM((rb, count, tile), F32),
            ],
            compiler_params=params(),
        )(tile_rows, tile_cols, tokens, gain2, gathered.reshape(number, tile, tile), cotangent)

        gain_grad = pl.pallas_call(
            functools.partial(gain_kernel, steps),
            out_shape=jax.ShapeDtypeStruct((rb, tile), F32),
            in_specs=[vmem],
            out_specs=vmem,
            scratch_shapes=[
                pltpu.VMEM((len(steps) + 1, rb, tile), F32),
                pltpu.VMEM((len(steps), rb, tile), F32),
                dma((len(steps),)), dma((len(steps),)),
            ],
            compiler_params=params(collective_id=1, has_side_effects=True),
        )(gain_part)
        return (projected, token_grad, tile_grad, gain_grad.reshape(width))

    data = P(("fsdp", "dp"), None)
    return jax.shard_map(
        shards,
        mesh=mesh,
        in_specs=(data, P(), P("fsdp", None, None), P(), P(), data),
        out_specs=(data, data, P("fsdp", None, None), P()),
        check_vma=False,
    )
```

```python
import functools

import jax
import jax.numpy as jnp
from jax import lax
from jax.experimental import pallas as pl
from jax.experimental.pallas import tpu as pltpu
from jax.sharding import PartitionSpec as P

MESH = pl.DeviceIdType.MESH
F32 = jnp.float32
BF16 = jnp.bfloat16
UNROLL = 8


def remote(src, dst, send, recv, f, d):
    return pltpu.make_async_remote_copy(
        src_ref=src, dst_ref=dst, send_sem=send, recv_sem=recv,
        device_id={"fsdp": f, "dp": d}, device_id_type=MESH,
    )


def row_scale(tok_ref, width, tile):
    total = jnp.zeros((tok_ref.shape[0], tile), F32)
    for b in range(width // tile):
        x = tok_ref[:, b * tile:(b + 1) * tile].astype(F32)
        total = total + x * x
    mean = jnp.sum(total, axis=-1, keepdims=True) / width
    return lax.rsqrt(mean + 1e-05)


def grads_kernel(rows_ref, cols_ref, tok_ref, gain_ref, cot_ref, part_ref, normed_t):
    number, tile = part_ref.shape[0], part_ref.shape[1]
    width = tok_ref.shape[1]
    scale = row_scale(tok_ref, width, tile)
    for b in range(width // tile):
        at = slice(b * tile, (b + 1) * tile)
        x = tok_ref[:, at].astype(F32)
        normed_t[b] = (x * scale * gain_ref[:, at]).T.astype(BF16)

    def body(i, carry):
        terms = []
        for u in range(UNROLL):
            k = i * UNROLL + u
            col = pl.multiple_of(cols_ref[k] * tile, tile)
            terms.append(jnp.dot(normed_t[rows_ref[k]], cot_ref[:, pl.ds(col, tile)], preferred_element_type=F32))
        for u in range(UNROLL):
            part_ref[i * UNROLL + u] = terms[u].astype(BF16)
        return carry

    lax.fori_loop(0, number // UNROLL, body, 0)


def comm_kernel(
    A, tiles_ref, part_ref, ag, out_ref,
    rc, ry, rz, xs, rx,
    lsem, cs, cr, ys, yr, zs, zr, xss, xrs, fs, fr,
    ays, ayr, azs, azr, axs, axr, acs, acr,
):
    f, d = lax.axis_index("fsdp"), lax.axis_index("dp")
    z, y = f // 2, f % 2
    x, c = d // 2, d % 2
    fy = z * 2 + (1 - y)
    dc = x * 2 + (1 - c)
    dx = (1 - x) * 2 + c
    dxc = (1 - x) * 2 + (1 - c)
    group = tiles_ref.shape[0]
    h, q = group // 2, group // 4
    has_left, has_right = z > 0, z < A - 1

    barrier = pltpu.get_barrier_semaphore()

    def greet(ff, dd):
        pl.semaphore_signal(barrier, inc=1, device_id={"fsdp": ff, "dp": dd}, device_id_type=MESH)

    greet(f, dc)
    greet(f, dx)
    greet(fy, d)
    pl.when(has_left)(lambda: greet(f - 2, d))
    pl.when(has_right)(lambda: greet(f + 2, d))
    pl.semaphore_wait(barrier, 3 + has_left.astype(jnp.int32) + has_right.astype(jnp.int32))

    def quarter(fb, dd):
        return ag.at[fb, pl.ds(dd * q, q)]

    def to_core(b, yy):
        fb = b * 2 + yy
        return remote(part_ref.at[fb, pl.ds((1 - c) * h, h)], rc.at[fb], cs.at[fb], cr.at[fb], f, dc)

    def to_y(b):
        return remote(rc.at[b * 2 + 1 - y], ry.at[b], ys.at[b], yr.at[b], fy, d)

    def to_right(b):
        return remote(rc.at[b * 2 + y], rz.at[b], zs.at[b], zr.at[b], f + 2, d)

    def to_left(b):
        slot = jnp.where(b == z - 1, A, b)
        return remote(rc.at[b * 2 + y], rz.at[slot], zs.at[b], zr.at[slot], f - 2, d)

    def arrived(slot):
        remote(rz.at[slot], rz.at[slot], zs.at[0], zr.at[slot], fy, d).wait_recv()

    own = tiles_ref.at[pl.ds(d * q, q)]
    own_y = remote(own, quarter(f, d), ays, ayr, fy, d)

    def ag_left(fb, src):
        return remote(src, quarter(fb, d), azs.at[0, fb], azr.at[fb], f - 2, d)

    def ag_right(fb, src):
        return remote(src, quarter(fb, d), azs.at[1, fb], azr.at[fb], f + 2, d)

    def ag_x(fb):
        return remote(quarter(fb, d), quarter(fb, d), axs.at[fb], axr.at[fb], f, dx)

    def ag_core(fb, which):
        dd = d if which == 0 else dx
        return remote(quarter(fb, dd), quarter(fb, dd), acs.at[which, fb], acr.at[which, fb], f, dc)

    def ag_landed(fb, dd, sem):
        remote(quarter(fb, dd), quarter(fb, dd), ays, sem, fy, d).wait_recv()

    def spread(fb):
        ag_x(fb).start()
        ag_core(fb, 0).start()

    own_y.start()
    pl.when(has_left)(lambda: ag_left(f, own).start())
    pl.when(has_right)(lambda: ag_right(f, own).start())
    keep = pltpu.make_async_copy(tiles_ref, ag.at[f], lsem)
    keep.start()

    after, before = A - 1 - z, z
    more_after = after >= before
    alone = jnp.where(more_after, after - before, before - after)
    paired = jnp.where(more_after, before, after)

    def order(i):
        j = i - alone
        step = paired - j // 2
        pair = jnp.where(j % 2 == 0, z + step, z - step)
        return jnp.where(i < alone, jnp.where(more_after, A - 1 - i, i), pair)

    def halves(fb):
        return part_ref[fb, pl.ds(c * h, h)].astype(F32) + rc[fb].astype(F32)

    def give_y(b):
        fb = b * 2 + 1 - y
        to_core(b, 1 - y).wait_recv()
        rc[fb] = halves(fb).astype(BF16)
        to_y(b).start()

    for i in range(A):
        to_core(order(i), 1 - y).start()
    for i in range(A):
        to_core(order(i), y).start()
    for i in range(A):
        give_y(order(i))
        if i == 0:
            ag_landed(fy, d, ayr)
            pl.when(has_left)(lambda: ag_left(fy, quarter(fy, d)).start())
            pl.when(has_right)(lambda: ag_right(fy, quarter(fy, d)).start())
            spread(fy)

    def summed(b):
        to_core(b, y).wait_recv()
        to_y(b).wait_recv()
        return halves(b * 2 + y) + ry[b].astype(F32)

    def gather_from_left(s):
        b = z - s
        for yy in range(2):
            fb = b * 2 + yy
            ag_landed(fb, d, azr.at[fb])
            pl.when(has_right)(lambda: ag_right(fb, quarter(fb, d)).start())
            spread(fb)

    def gather_from_right(s):
        b = z + s
        for yy in range(2):
            fb = b * 2 + yy
            ag_landed(fb, d, azr.at[fb])
            pl.when(has_left)(lambda: ag_left(fb, quarter(fb, d)).start())
            spread(fb)

    def send_sum_right(s):
        b = z + s
        fb = b * 2 + y
        rc[fb] = summed(b).astype(BF16)

        @pl.when(has_left)
        def _():
            arrived(b)
            rc[fb] = (rc[fb].astype(F32) + rz[b].astype(F32)).astype(BF16)

        to_right(b).start()

    def send_sum_left(s):
        b = z - s
        fb = b * 2 + y
        rc[fb] = summed(b).astype(BF16)

        @pl.when(has_right)
        def _():
            arrived(b)
            rc[fb] = (rc[fb].astype(F32) + rz[b].astype(F32)).astype(BF16)

        to_left(b).start()

    def gather(s):
        if s < A:
            pl.when(z - s >= 0)(functools.partial(gather_from_left, s))
            pl.when(z + s < A)(functools.partial(gather_from_right, s))

    gather(1)
    for s in range(1, A):
        far = A - s
        gather(s + 1)
        pl.when(z + far < A)(functools.partial(send_sum_right, far))
        pl.when(z - far >= 0)(functools.partial(send_sum_left, far))

    mine = pl.ds(c * h, h)
    out_ref[mine] = summed(z)

    @pl.when(has_left)
    def _():
        arrived(z)
        out_ref[mine] = out_ref[mine] + rz[z].astype(F32)

    @pl.when(has_right)
    def _():
        arrived(A)
        out_ref[mine] = out_ref[mine] + rz[A].astype(F32)

    xs[...] = out_ref[mine].astype(BF16)
    across = remote(xs, rx, xss, xrs, f, dx)
    across.start()

    def visit(fn):
        fn(fy)
        for s in range(1, A):
            @pl.when(z - s >= 0)
            def _():
                fn((z - s) * 2)
                fn((z - s) * 2 + 1)

            @pl.when(z + s < A)
            def _():
                fn((z + s) * 2)
                fn((z + s) * 2 + 1)

    def relay(fb):
        ag_landed(fb, dx, axr.at[fb])
        ag_core(fb, 1).start()

    visit(relay)

    across.wait_recv()
    out_ref[mine] = xs[...].astype(F32) + rx[...].astype(F32)
    last = remote(out_ref.at[mine], out_ref.at[mine], fs, fr, f, dc)
    last.start()

    def finish(fb):
        ag_landed(fb, dc, acr.at[0, fb])
        ag_landed(fb, dxc, acr.at[1, fb])
        ag_x(fb).wait_send()
        ag_core(fb, 0).wait_send()
        ag_core(fb, 1).wait_send()

    visit(finish)

    other = out_ref.at[pl.ds((1 - c) * h, h)]
    remote(other, other, fs, fr, f, dc).wait_recv()
    last.wait_send()
    across.wait_send()
    keep.wait()
    own_y.wait_send()
    for fb in (f, fy):
        pl.when(has_left)(lambda: ag_left(fb, own).wait_send())
        pl.when(has_right)(lambda: ag_right(fb, own).wait_send())
    for b in range(A):
        to_core(b, 0).wait_send()
        to_core(b, 1).wait_send()
        to_y(b).wait_send()
    for s in range(1, A):
        @pl.when(z + s < A)
        def _():
            to_right(z + s).wait_send()
            for yy in range(2):
                pl.when(has_left)(lambda: ag_left((z + s) * 2 + yy, own).wait_send())

        @pl.when(z - s >= 0)
        def _():
            to_left(z - s).wait_send()
            for yy in range(2):
                pl.when(has_right)(lambda: ag_right((z - s) * 2 + yy, own).wait_send())


def apply_kernel(
    rows_ref, cols_ref, tok_ref, gain_ref, tiles_ref, cot_ref, proj_ref, tgrad_ref, ggrad_ref,
    normed, outsum, back,
):
    number, tile = tiles_ref.shape[0], tiles_ref.shape[1]
    count, width = tok_ref.shape
    scale = row_scale(tok_ref, width, tile)
    for b in range(width // tile):
        at = slice(b * tile, (b + 1) * tile)
        normed[b] = (tok_ref[:, at].astype(F32) * scale * gain_ref[:, at]).astype(BF16)
        back[b] = jnp.zeros((count, tile), F32)

    def clear(b, carry):
        outsum[b] = jnp.zeros((count, tile), F32)
        return carry

    lax.fori_loop(0, outsum.shape[0], clear, 0)

    def body(i, carry):
        forward, backward, places = [], [], []
        for u in range(UNROLL):
            k = i * UNROLL + u
            r, c = rows_ref[k], cols_ref[k]
            places.append((r, c))
            weight = tiles_ref[k]
            g = cot_ref[:, pl.ds(pl.multiple_of(c * tile, tile), tile)]
            forward.append(jnp.dot(normed[r], weight, preferred_element_type=F32))
            backward.append(lax.dot_general(g, weight, (((1,), (1,)), ((), ())), preferred_element_type=F32))
        for u in range(UNROLL):
            r, c = places[u]
            outsum[c] = outsum[c] + forward[u]
            back[r] = back[r] + backward[u]
        return carry

    lax.fori_loop(0, number // UNROLL, body, 0)

    inner = jnp.zeros((count, tile), F32)
    for b in range(width // tile):
        at = slice(b * tile, (b + 1) * tile)
        x = tok_ref[:, at].astype(F32)
        dn = back[b]
        inner = inner + x * gain_ref[:, at] * dn
        ggrad_ref[b:b + 1, :] = jnp.sum(dn * x * scale, axis=0, keepdims=True)
    inner = jnp.sum(inner, axis=-1, keepdims=True) / width
    weight = scale * scale * scale * inner
    for b in range(width // tile):
        at = slice(b * tile, (b + 1) * tile)
        x = tok_ref[:, at].astype(F32)
        tgrad_ref[:, at] = (scale * gain_ref[:, at] * back[b] - x * weight).astype(BF16)
    for b in range(outsum.shape[0]):
        proj_ref[:, b * tile:(b + 1) * tile] = outsum[b].astype(BF16)


def gain_kernel(nf, nd, part_ref, out_ref, got_d, got_f, send_d, recv_d, send_f, recv_f):
    f, d = lax.axis_index("fsdp"), lax.axis_index("dp")
    barrier = pltpu.get_barrier_semaphore()
    for o in range(1, nd):
        pl.semaphore_signal(barrier, inc=1, device_id={"fsdp": f, "dp": (d + o) % nd}, device_id_type=MESH)
    for o in range(1, nf):
        pl.semaphore_signal(barrier, inc=1, device_id={"fsdp": (f + o) % nf, "dp": d}, device_id_type=MESH)
    pl.semaphore_wait(barrier, nd - 1 + nf - 1)

    def exchange(n, me, got, send, recv, place):
        out = [remote(got.at[me], got.at[me], send.at[o], recv.at[me], *place((me + o) % n)) for o in range(1, n)]
        for copy in out:
            copy.start()
        for o in range(1, n):
            there = (me + o) % n
            remote(got.at[there], got.at[there], send.at[o], recv.at[there], *place(there)).wait_recv()
        total = got[0]
        for k in range(1, n):
            total = total + got[k]
        for copy in out:
            copy.wait_send()
        return total

    got_d[d] = part_ref[...]
    got_f[f] = exchange(nd, d, got_d, send_d, recv_d, lambda dd: (f, dd))
    out_ref[...] = exchange(nf, f, got_f, send_f, recv_f, lambda ff: (ff, d))


def solution(mesh):
    nf, nd = mesh.shape["fsdp"], mesh.shape["dp"]
    A = nf // 2
    vmem = pl.BlockSpec(memory_space=pltpu.VMEM)
    smem = pl.BlockSpec(memory_space=pltpu.SMEM)
    anywhere = pl.BlockSpec(memory_space=pl.ANY)
    dma = pltpu.SemaphoreType.DMA
    params = functools.partial(pltpu.CompilerParams, vmem_limit_bytes=60 * 2**20)

    def shards(tokens, gain, tiles, tile_rows, tile_cols, cotangent):
        count, width = tokens.shape
        group, tile, _ = tiles.shape
        number = group * nf
        rb, cb = width // tile, cotangent.shape[1] // tile
        h = group // 2
        gain2 = gain.reshape(1, width)

        part = pl.pallas_call(
            grads_kernel,
            out_shape=jax.ShapeDtypeStruct((number, tile, tile), BF16),
            in_specs=[smem, smem, vmem, vmem, vmem],
            out_specs=vmem,
            scratch_shapes=[pltpu.VMEM((rb, tile, count), BF16)],
            compiler_params=params(),
        )(tile_rows, tile_cols, tokens, gain2, cotangent)

        gathered, tile_grad = pl.pallas_call(
            functools.partial(comm_kernel, A),
            out_shape=(
                jax.ShapeDtypeStruct((nf, group, tile, tile), BF16),
                jax.ShapeDtypeStruct((group, tile, tile), F32),
            ),
            in_specs=[anywhere, vmem],
            out_specs=(anywhere, vmem),
            scratch_shapes=[
                pltpu.VMEM((nf, h, tile, tile), BF16),
                pltpu.VMEM((A, h, tile, tile), BF16),
                pltpu.VMEM((A + 1, h, tile, tile), BF16),
                pltpu.VMEM((h, tile, tile), BF16),
                pltpu.VMEM((h, tile, tile), BF16),
                dma,
                dma((nf,)), dma((nf,)),
                dma((A,)), dma((A,)),
                dma((A,)), dma((A + 1,)),
                dma, dma, dma, dma,
                dma, dma,
                dma((2, nf)), dma((nf,)),
                dma((nf,)), dma((nf,)),
                dma((2, nf)), dma((2, nf)),
            ],
            compiler_params=params(collective_id=0, has_side_effects=True),
        )(tiles, part.reshape(nf, group, tile, tile))

        projected, token_grad, gain_part = pl.pallas_call(
            apply_kernel,
            out_shape=(
                jax.ShapeDtypeStruct(cotangent.shape, BF16),
                jax.ShapeDtypeStruct(tokens.shape, BF16),
                jax.ShapeDtypeStruct((rb, tile), F32),
            ),
            in_specs=[smem, smem, vmem, vmem, vmem, vmem],
            out_specs=(vmem, vmem, vmem),
            scratch_shapes=[
                pltpu.VMEM((rb, count, tile), BF16),
                pltpu.VMEM((cb, count, tile), F32),
                pltpu.VMEM((rb, count, tile), F32),
            ],
            compiler_params=params(),
        )(tile_rows, tile_cols, tokens, gain2, gathered.reshape(number, tile, tile), cotangent)

        gain_grad = pl.pallas_call(
            functools.partial(gain_kernel, nf, nd),
            out_shape=jax.ShapeDtypeStruct((rb, tile), F32),
            in_specs=[vmem],
            out_specs=vmem,
            scratch_shapes=[
                pltpu.VMEM((nd, rb, tile), F32),
                pltpu.VMEM((nf, rb, tile), F32),
                dma((nd,)), dma((nd,)), dma((nf,)), dma((nf,)),
            ],
            compiler_params=params(collective_id=1, has_side_effects=True),
        )(gain_part)
        return (projected, token_grad, tile_grad, gain_grad.reshape(width))

    data = P(("fsdp", "dp"), None)
    return jax.shard_map(
        shards,
        mesh=mesh,
        in_specs=(data, P(), P("fsdp", None, None), P(), P(), data),
        out_specs=(data, data, P("fsdp", None, None), P()),
        check_vma=False,
    )
```

```python
import functools

import jax
import jax.numpy as jnp
from jax import lax
from jax.experimental import pallas as pl
from jax.experimental.pallas import tpu as pltpu
from jax.sharding import PartitionSpec as P

MESH = pl.DeviceIdType.MESH
F32 = jnp.float32
BF16 = jnp.bfloat16
UNROLL = 8


def remote(src, dst, send, recv, f, d):
    return pltpu.make_async_remote_copy(
        src_ref=src, dst_ref=dst, send_sem=send, recv_sem=recv,
        device_id={"fsdp": f, "dp": d}, device_id_type=MESH,
    )


def row_scale(tok_ref, width, tile):
    total = jnp.zeros((tok_ref.shape[0], tile), F32)
    for b in range(width // tile):
        x = tok_ref[:, b * tile:(b + 1) * tile].astype(F32)
        total = total + x * x
    mean = jnp.sum(total, axis=-1, keepdims=True) / width
    return lax.rsqrt(mean + 1e-05)


def comm_kernel(
    A, rows_ref, cols_ref, tok_ref, gain_ref, cot_ref, tiles_ref, ag, out_ref,
    normed_t, cot_blocks, part_ref, rc, ry, rz, xs, rx,
    lsem, cs, cr, ys, yr, zs, zr, xss, xrs, fs, fr,
    ays, ayr, azs, azr, axs, axr, acs, acr,
):
    f, d = lax.axis_index("fsdp"), lax.axis_index("dp")
    z, y = f // 2, f % 2
    x, c = d // 2, d % 2
    fy = z * 2 + (1 - y)
    dc = x * 2 + (1 - c)
    dx = (1 - x) * 2 + c
    dxc = (1 - x) * 2 + (1 - c)
    group = tiles_ref.shape[0]
    h, q = group // 2, group // 4
    tile, width = tiles_ref.shape[1], tok_ref.shape[1]
    has_left, has_right = z > 0, z < A - 1

    barrier = pltpu.get_barrier_semaphore()

    def greet(ff, dd):
        pl.semaphore_signal(barrier, inc=1, device_id={"fsdp": ff, "dp": dd}, device_id_type=MESH)

    greet(f, dc)
    greet(f, dx)
    greet(fy, d)
    pl.when(has_left)(lambda: greet(f - 2, d))
    pl.when(has_right)(lambda: greet(f + 2, d))
    pl.semaphore_wait(barrier, 3 + has_left.astype(jnp.int32) + has_right.astype(jnp.int32))

    def quarter(fb, dd):
        return ag.at[fb, pl.ds(dd * q, q)]

    def to_core(b, yy):
        fb = b * 2 + yy
        return remote(part_ref.at[fb, pl.ds((1 - c) * h, h)], rc.at[fb], cs.at[fb], cr.at[fb], f, dc)

    def to_y(b):
        return remote(rc.at[b * 2 + 1 - y], ry.at[b], ys.at[b], yr.at[b], fy, d)

    def to_right(b):
        return remote(rc.at[b * 2 + y], rz.at[b], zs.at[b], zr.at[b], f + 2, d)

    def to_left(b):
        slot = jnp.where(b == z - 1, A, b)
        return remote(rc.at[b * 2 + y], rz.at[slot], zs.at[b], zr.at[slot], f - 2, d)

    def arrived(slot):
        remote(rz.at[slot], rz.at[slot], zs.at[0], zr.at[slot], fy, d).wait_recv()

    own = tiles_ref.at[pl.ds(d * q, q)]
    own_y = remote(own, quarter(f, d), ays, ayr, fy, d)

    def ag_left(fb, src):
        return remote(src, quarter(fb, d), azs.at[0, fb], azr.at[fb], f - 2, d)

    def ag_right(fb, src):
        return remote(src, quarter(fb, d), azs.at[1, fb], azr.at[fb], f + 2, d)

    def ag_x(fb):
        return remote(quarter(fb, d), quarter(fb, d), axs.at[fb], axr.at[fb], f, dx)

    def ag_core(fb, which):
        dd = d if which == 0 else dx
        return remote(quarter(fb, dd), quarter(fb, dd), acs.at[which, fb], acr.at[which, fb], f, dc)

    def ag_landed(fb, dd, sem):
        remote(quarter(fb, dd), quarter(fb, dd), ays, sem, fy, d).wait_recv()

    def spread(fb):
        ag_x(fb).start()
        ag_core(fb, 0).start()

    own_y.start()
    pl.when(has_left)(lambda: ag_left(f, own).start())
    pl.when(has_right)(lambda: ag_right(f, own).start())
    keep = pltpu.make_async_copy(tiles_ref, ag.at[f], lsem)
    keep.start()

    after, before = A - 1 - z, z
    more_after = after >= before
    alone = jnp.where(more_after, after - before, before - after)
    paired = jnp.where(more_after, before, after)

    def order(i):
        j = i - alone
        step = paired - j // 2
        pair = jnp.where(j % 2 == 0, z + step, z - step)
        return jnp.where(i < alone, jnp.where(more_after, A - 1 - i, i), pair)

    scale = row_scale(tok_ref, width, tile)
    for b in range(width // tile):
        at = slice(b * tile, (b + 1) * tile)
        normed_t[b] = (tok_ref[:, at].astype(F32) * scale * gain_ref[:, at]).T.astype(BF16)

    for b in range(cot_ref.shape[1] // tile):
        cot_blocks[b] = cot_ref[:, b * tile:(b + 1) * tile]

    def terms(b, yy):
        fb = b * 2 + yy

        def body(i, carry):
            found = []
            for u in range(UNROLL):
                k = fb * group + i * UNROLL + u
                found.append(jnp.dot(normed_t[rows_ref[k]], cot_blocks[cols_ref[k]], preferred_element_type=F32))
            for u in range(UNROLL):
                part_ref[fb, i * UNROLL + u] = found[u].astype(BF16)
            return carry

        lax.fori_loop(0, group // UNROLL, body, 0)
        to_core(b, yy).start()

    def halves(fb):
        return part_ref[fb, pl.ds(c * h, h)].astype(F32) + rc[fb].astype(F32)

    def give_y(b):
        fb = b * 2 + 1 - y
        to_core(b, 1 - y).wait_recv()
        rc[fb] = halves(fb).astype(BF16)
        to_y(b).start()

    for i in range(A):
        terms(order(i), 1 - y)
        if i == 0:
            ag_landed(fy, d, ayr)
            pl.when(has_left)(lambda: ag_left(fy, quarter(fy, d)).start())
            pl.when(has_right)(lambda: ag_right(fy, quarter(fy, d)).start())
            spread(fy)
        else:
            give_y(order(i - 1))

    def summed(b):
        to_core(b, y).wait_recv()
        to_y(b).wait_recv()
        return halves(b * 2 + y) + ry[b].astype(F32)

    def gather_from_left(s):
        b = z - s
        for yy in range(2):
            fb = b * 2 + yy
            ag_landed(fb, d, azr.at[fb])
            pl.when(has_right)(lambda: ag_right(fb, quarter(fb, d)).start())
            spread(fb)

    def gather_from_right(s):
        b = z + s
        for yy in range(2):
            fb = b * 2 + yy
            ag_landed(fb, d, azr.at[fb])
            pl.when(has_left)(lambda: ag_left(fb, quarter(fb, d)).start())
            spread(fb)

    def send_sum_right(s):
        b = z + s
        fb = b * 2 + y
        rc[fb] = summed(b).astype(BF16)

        @pl.when(has_left)
        def _():
            arrived(b)
            rc[fb] = (rc[fb].astype(F32) + rz[b].astype(F32)).astype(BF16)

        to_right(b).start()

    def send_sum_left(s):
        b = z - s
        fb = b * 2 + y
        rc[fb] = summed(b).astype(BF16)

        @pl.when(has_right)
        def _():
            arrived(b)
            rc[fb] = (rc[fb].astype(F32) + rz[b].astype(F32)).astype(BF16)

        to_left(b).start()

    def gather(s):
        if s < A:
            pl.when(z - s >= 0)(functools.partial(gather_from_left, s))
            pl.when(z + s < A)(functools.partial(gather_from_right, s))

    terms(order(0), y)
    give_y(order(A - 1))
    gather(1)
    for i in range(1, A):
        terms(order(i), y)
    for s in range(1, A):
        far = A - s
        gather(s + 1)
        pl.when(z + far < A)(functools.partial(send_sum_right, far))
        pl.when(z - far >= 0)(functools.partial(send_sum_left, far))

    mine = pl.ds(c * h, h)
    out_ref[mine] = summed(z)

    @pl.when(has_left)
    def _():
        arrived(z)
        out_ref[mine] = out_ref[mine] + rz[z].astype(F32)

    @pl.when(has_right)
    def _():
        arrived(A)
        out_ref[mine] = out_ref[mine] + rz[A].astype(F32)

    xs[...] = out_ref[mine].astype(BF16)
    across = remote(xs, rx, xss, xrs, f, dx)
    across.start()

    def visit(fn):
        fn(fy)
        for s in range(1, A):
            @pl.when(z - s >= 0)
            def _():
                fn((z - s) * 2)
                fn((z - s) * 2 + 1)

            @pl.when(z + s < A)
            def _():
                fn((z + s) * 2)
                fn((z + s) * 2 + 1)

    def relay(fb):
        ag_landed(fb, dx, axr.at[fb])
        ag_core(fb, 1).start()

    visit(relay)

    across.wait_recv()
    out_ref[mine] = xs[...].astype(F32) + rx[...].astype(F32)
    last = remote(out_ref.at[mine], out_ref.at[mine], fs, fr, f, dc)
    last.start()

    def finish(fb):
        ag_landed(fb, dc, acr.at[0, fb])
        ag_landed(fb, dxc, acr.at[1, fb])
        ag_x(fb).wait_send()
        ag_core(fb, 0).wait_send()
        ag_core(fb, 1).wait_send()

    visit(finish)

    other = out_ref.at[pl.ds((1 - c) * h, h)]
    remote(other, other, fs, fr, f, dc).wait_recv()
    last.wait_send()
    across.wait_send()
    keep.wait()
    own_y.wait_send()
    for fb in (f, fy):
        pl.when(has_left)(lambda: ag_left(fb, own).wait_send())
        pl.when(has_right)(lambda: ag_right(fb, own).wait_send())
    for b in range(A):
        to_core(b, 0).wait_send()
        to_core(b, 1).wait_send()
        to_y(b).wait_send()
    for s in range(1, A):
        @pl.when(z + s < A)
        def _():
            to_right(z + s).wait_send()
            for yy in range(2):
                pl.when(has_left)(lambda: ag_left((z + s) * 2 + yy, own).wait_send())

        @pl.when(z - s >= 0)
        def _():
            to_left(z - s).wait_send()
            for yy in range(2):
                pl.when(has_right)(lambda: ag_right((z - s) * 2 + yy, own).wait_send())


def apply_kernel(
    rows_ref, cols_ref, tok_ref, gain_ref, tiles_ref, cot_ref, proj_ref, tgrad_ref, ggrad_ref,
    normed, outsum, back,
):
    number, tile = tiles_ref.shape[0], tiles_ref.shape[1]
    count, width = tok_ref.shape
    scale = row_scale(tok_ref, width, tile)
    for b in range(width // tile):
        at = slice(b * tile, (b + 1) * tile)
        normed[b] = (tok_ref[:, at].astype(F32) * scale * gain_ref[:, at]).astype(BF16)
        back[b] = jnp.zeros((count, tile), F32)

    def clear(b, carry):
        outsum[b] = jnp.zeros((count, tile), F32)
        return carry

    lax.fori_loop(0, outsum.shape[0], clear, 0)

    def body(i, carry):
        forward, backward, places = [], [], []
        for u in range(UNROLL):
            k = i * UNROLL + u
            r, c = rows_ref[k], cols_ref[k]
            places.append((r, c))
            weight = tiles_ref[k]
            g = cot_ref[:, pl.ds(pl.multiple_of(c * tile, tile), tile)]
            forward.append(jnp.dot(normed[r], weight, preferred_element_type=F32))
            backward.append(lax.dot_general(g, weight, (((1,), (1,)), ((), ())), preferred_element_type=F32))
        for u in range(UNROLL):
            r, c = places[u]
            outsum[c] = outsum[c] + forward[u]
            back[r] = back[r] + backward[u]
        return carry

    lax.fori_loop(0, number // UNROLL, body, 0)

    inner = jnp.zeros((count, tile), F32)
    for b in range(width // tile):
        at = slice(b * tile, (b + 1) * tile)
        x = tok_ref[:, at].astype(F32)
        dn = back[b]
        inner = inner + x * gain_ref[:, at] * dn
        ggrad_ref[b:b + 1, :] = jnp.sum(dn * x * scale, axis=0, keepdims=True)
    inner = jnp.sum(inner, axis=-1, keepdims=True) / width
    weight = scale * scale * scale * inner
    for b in range(width // tile):
        at = slice(b * tile, (b + 1) * tile)
        x = tok_ref[:, at].astype(F32)
        tgrad_ref[:, at] = (scale * gain_ref[:, at] * back[b] - x * weight).astype(BF16)
    for b in range(outsum.shape[0]):
        proj_ref[:, b * tile:(b + 1) * tile] = outsum[b].astype(BF16)


def gain_kernel(nf, nd, part_ref, out_ref, got_d, got_f, send_d, recv_d, send_f, recv_f):
    f, d = lax.axis_index("fsdp"), lax.axis_index("dp")
    barrier = pltpu.get_barrier_semaphore()
    for o in range(1, nd):
        pl.semaphore_signal(barrier, inc=1, device_id={"fsdp": f, "dp": (d + o) % nd}, device_id_type=MESH)
    for o in range(1, nf):
        pl.semaphore_signal(barrier, inc=1, device_id={"fsdp": (f + o) % nf, "dp": d}, device_id_type=MESH)
    pl.semaphore_wait(barrier, nd - 1 + nf - 1)

    def exchange(n, me, got, send, recv, place):
        out = [remote(got.at[me], got.at[me], send.at[o], recv.at[me], *place((me + o) % n)) for o in range(1, n)]
        for copy in out:
            copy.start()
        for o in range(1, n):
            there = (me + o) % n
            remote(got.at[there], got.at[there], send.at[o], recv.at[there], *place(there)).wait_recv()
        total = got[0]
        for k in range(1, n):
            total = total + got[k]
        for copy in out:
            copy.wait_send()
        return total

    got_d[d] = part_ref[...]
    got_f[f] = exchange(nd, d, got_d, send_d, recv_d, lambda dd: (f, dd))
    out_ref[...] = exchange(nf, f, got_f, send_f, recv_f, lambda ff: (ff, d))


def solution(mesh):
    nf, nd = mesh.shape["fsdp"], mesh.shape["dp"]
    A = nf // 2
    vmem = pl.BlockSpec(memory_space=pltpu.VMEM)
    smem = pl.BlockSpec(memory_space=pltpu.SMEM)
    anywhere = pl.BlockSpec(memory_space=pl.ANY)
    dma = pltpu.SemaphoreType.DMA
    params = functools.partial(pltpu.CompilerParams, vmem_limit_bytes=60 * 2**20)

    def shards(tokens, gain, tiles, tile_rows, tile_cols, cotangent):
        count, width = tokens.shape
        group, tile, _ = tiles.shape
        number = group * nf
        rb, cb = width // tile, cotangent.shape[1] // tile
        h = group // 2
        gain2 = gain.reshape(1, width)

        gathered, tile_grad = pl.pallas_call(
            functools.partial(comm_kernel, A),
            out_shape=(
                jax.ShapeDtypeStruct((nf, group, tile, tile), BF16),
                jax.ShapeDtypeStruct((group, tile, tile), F32),
            ),
            in_specs=[smem, smem, vmem, vmem, vmem, anywhere],
            out_specs=(anywhere, vmem),
            scratch_shapes=[
                pltpu.VMEM((rb, tile, count), BF16),
                pltpu.VMEM((cb, count, tile), BF16),
                pltpu.VMEM((nf, group, tile, tile), BF16),
                pltpu.VMEM((nf, h, tile, tile), BF16),
                pltpu.VMEM((A, h, tile, tile), BF16),
                pltpu.VMEM((A + 1, h, tile, tile), BF16),
                pltpu.VMEM((h, tile, tile), BF16),
                pltpu.VMEM((h, tile, tile), BF16),
                dma,
                dma((nf,)), dma((nf,)),
                dma((A,)), dma((A,)),
                dma((A,)), dma((A + 1,)),
                dma, dma, dma, dma,
                dma, dma,
                dma((2, nf)), dma((nf,)),
                dma((nf,)), dma((nf,)),
                dma((2, nf)), dma((2, nf)),
            ],
            compiler_params=params(collective_id=0, has_side_effects=True),
        )(tile_rows, tile_cols, tokens, gain2, cotangent, tiles)

        projected, token_grad, gain_part = pl.pallas_call(
            apply_kernel,
            out_shape=(
                jax.ShapeDtypeStruct(cotangent.shape, BF16),
                jax.ShapeDtypeStruct(tokens.shape, BF16),
                jax.ShapeDtypeStruct((rb, tile), F32),
            ),
            in_specs=[smem, smem, vmem, vmem, vmem, vmem],
            out_specs=(vmem, vmem, vmem),
            scratch_shapes=[
                pltpu.VMEM((rb, count, tile), BF16),
                pltpu.VMEM((cb, count, tile), F32),
                pltpu.VMEM((rb, count, tile), F32),
            ],
            compiler_params=params(),
        )(tile_rows, tile_cols, tokens, gain2, gathered.reshape(number, tile, tile), cotangent)

        gain_grad = pl.pallas_call(
            functools.partial(gain_kernel, nf, nd),
            out_shape=jax.ShapeDtypeStruct((rb, tile), F32),
            in_specs=[vmem],
            out_specs=vmem,
            scratch_shapes=[
                pltpu.VMEM((nd, rb, tile), F32),
                pltpu.VMEM((nf, rb, tile), F32),
                dma((nd,)), dma((nd,)), dma((nf,)), dma((nf,)),
            ],
            compiler_params=params(collective_id=1, has_side_effects=True),
        )(gain_part)
        return (projected, token_grad, tile_grad, gain_grad.reshape(width))

    data = P(("fsdp", "dp"), None)
    return jax.shard_map(
        shards,
        mesh=mesh,
        in_specs=(data, P(), P("fsdp", None, None), P(), P(), data),
        out_specs=(data, data, P("fsdp", None, None), P()),
        check_vma=False,
    )
```

```python
import functools

import jax
import jax.numpy as jnp
from jax import lax
from jax.experimental import pallas as pl
from jax.experimental.pallas import tpu as pltpu
from jax.sharding import PartitionSpec as P

MESH = pl.DeviceIdType.MESH
F32 = jnp.float32
BF16 = jnp.bfloat16
UNROLL = 8


def remote(src, dst, send, recv, f, d):
    return pltpu.make_async_remote_copy(
        src_ref=src, dst_ref=dst, send_sem=send, recv_sem=recv,
        device_id={"fsdp": f, "dp": d}, device_id_type=MESH,
    )


def row_scale(tok_ref, width, tile):
    total = jnp.zeros((tok_ref.shape[0], tile), F32)
    for b in range(width // tile):
        x = tok_ref[:, b * tile:(b + 1) * tile].astype(F32)
        total = total + x * x
    mean = jnp.sum(total, axis=-1, keepdims=True) / width
    return lax.rsqrt(mean + 1e-05)


def comm_kernel(
    A, rows_ref, cols_ref, tok_ref, gain_ref, cot_hbm, tiles_ref, ag, xs,
    cot_ref, out_ref, normed_t, cot_blocks, part_ref, rc, ry, rz,
    csem, lsem, cs, cr, ys, yr, zs, zr,
    ays, ayr, azs, azr, axs, axr, acs, acr,
):
    f, d = lax.axis_index("fsdp"), lax.axis_index("dp")
    z, y = f // 2, f % 2
    x, c = d // 2, d % 2
    fy = z * 2 + (1 - y)
    dc = x * 2 + (1 - c)
    dx = (1 - x) * 2 + c
    dxc = (1 - x) * 2 + (1 - c)
    group = tiles_ref.shape[0]
    h, q = group // 2, group // 4
    tile, width = tiles_ref.shape[1], tok_ref.shape[1]
    has_left, has_right = z > 0, z < A - 1
    fetch = pltpu.make_async_copy(cot_hbm, cot_ref, csem)
    fetch.start()

    barrier = pltpu.get_barrier_semaphore()

    def greet(ff, dd):
        pl.semaphore_signal(barrier, inc=1, device_id={"fsdp": ff, "dp": dd}, device_id_type=MESH)

    greet(f, dc)
    greet(f, dx)
    greet(fy, d)
    pl.when(has_left)(lambda: greet(f - 2, d))
    pl.when(has_right)(lambda: greet(f + 2, d))
    pl.semaphore_wait(barrier, 3 + has_left.astype(jnp.int32) + has_right.astype(jnp.int32))

    def quarter(fb, dd):
        return ag.at[fb, pl.ds(dd * q, q)]

    def to_core(b, yy):
        fb = b * 2 + yy
        return remote(part_ref.at[fb, pl.ds((1 - c) * h, h)], rc.at[fb], cs.at[fb], cr.at[fb], f, dc)

    def to_y(b):
        return remote(rc.at[b * 2 + 1 - y], ry.at[b], ys.at[b], yr.at[b], fy, d)

    def to_right(b):
        return remote(rc.at[b * 2 + y], rz.at[b], zs.at[b], zr.at[b], f + 2, d)

    def to_left(b):
        slot = jnp.where(b == z - 1, A, b)
        return remote(rc.at[b * 2 + y], rz.at[slot], zs.at[b], zr.at[slot], f - 2, d)

    def arrived(slot):
        remote(rz.at[slot], rz.at[slot], zs.at[0], zr.at[slot], fy, d).wait_recv()

    own = tiles_ref.at[pl.ds(d * q, q)]
    own_y = remote(own, quarter(f, d), ays, ayr, fy, d)

    def ag_left(fb, src):
        return remote(src, quarter(fb, d), azs.at[0, fb], azr.at[fb], f - 2, d)

    def ag_right(fb, src):
        return remote(src, quarter(fb, d), azs.at[1, fb], azr.at[fb], f + 2, d)

    def ag_x(fb):
        return remote(quarter(fb, d), quarter(fb, d), axs.at[fb], axr.at[fb], f, dx)

    def ag_core(fb, which):
        dd = d if which == 0 else dx
        return remote(quarter(fb, dd), quarter(fb, dd), acs.at[which, fb], acr.at[which, fb], f, dc)

    def ag_landed(fb, dd, sem):
        remote(quarter(fb, dd), quarter(fb, dd), ays, sem, fy, d).wait_recv()

    def spread(fb):
        ag_x(fb).start()
        ag_core(fb, 0).start()

    own_y.start()
    pl.when(has_left)(lambda: ag_left(f, own).start())
    pl.when(has_right)(lambda: ag_right(f, own).start())
    keep = pltpu.make_async_copy(tiles_ref, ag.at[f], lsem)
    keep.start()

    after, before = A - 1 - z, z
    more_after = after >= before
    alone = jnp.where(more_after, after - before, before - after)
    paired = jnp.where(more_after, before, after)

    def order(i):
        j = i - alone
        step = paired - j // 2
        pair = jnp.where(j % 2 == 0, z + step, z - step)
        return jnp.where(i < alone, jnp.where(more_after, A - 1 - i, i), pair)

    scale = row_scale(tok_ref, width, tile)
    for b in range(width // tile):
        at = slice(b * tile, (b + 1) * tile)
        normed_t[b] = (tok_ref[:, at].astype(F32) * scale * gain_ref[:, at]).T.astype(BF16)

    fetch.wait()
    for b in range(cot_ref.shape[1] // tile):
        cot_blocks[b] = cot_ref[:, b * tile:(b + 1) * tile]

    def terms(b, yy):
        fb = b * 2 + yy

        def body(i, carry):
            found = []
            for u in range(UNROLL):
                k = fb * group + i * UNROLL + u
                found.append(jnp.dot(normed_t[rows_ref[k]], cot_blocks[cols_ref[k]], preferred_element_type=F32))
            for u in range(UNROLL):
                part_ref[fb, i * UNROLL + u] = found[u].astype(BF16)
            return carry

        lax.fori_loop(0, group // UNROLL, body, 0)
        to_core(b, yy).start()

    def halves(fb):
        return part_ref[fb, pl.ds(c * h, h)].astype(F32) + rc[fb].astype(F32)

    def give_y(b):
        fb = b * 2 + 1 - y
        to_core(b, 1 - y).wait_recv()
        rc[fb] = halves(fb).astype(BF16)
        to_y(b).start()

    for i in range(A):
        terms(order(i), 1 - y)
        if i == 0:
            ag_landed(fy, d, ayr)
            pl.when(has_left)(lambda: ag_left(fy, quarter(fy, d)).start())
            pl.when(has_right)(lambda: ag_right(fy, quarter(fy, d)).start())
            spread(fy)
        else:
            give_y(order(i - 1))

    def summed(b):
        to_core(b, y).wait_recv()
        to_y(b).wait_recv()
        return halves(b * 2 + y) + ry[b].astype(F32)

    def gather_from_left(s):
        b = z - s
        for yy in range(2):
            fb = b * 2 + yy
            ag_landed(fb, d, azr.at[fb])
            pl.when(has_right)(lambda: ag_right(fb, quarter(fb, d)).start())
            spread(fb)

    def gather_from_right(s):
        b = z + s
        for yy in range(2):
            fb = b * 2 + yy
            ag_landed(fb, d, azr.at[fb])
            pl.when(has_left)(lambda: ag_left(fb, quarter(fb, d)).start())
            spread(fb)

    def send_sum_right(s):
        b = z + s
        fb = b * 2 + y
        rc[fb] = summed(b).astype(BF16)

        @pl.when(has_left)
        def _():
            arrived(b)
            rc[fb] = (rc[fb].astype(F32) + rz[b].astype(F32)).astype(BF16)

        to_right(b).start()

    def send_sum_left(s):
        b = z - s
        fb = b * 2 + y
        rc[fb] = summed(b).astype(BF16)

        @pl.when(has_right)
        def _():
            arrived(b)
            rc[fb] = (rc[fb].astype(F32) + rz[b].astype(F32)).astype(BF16)

        to_left(b).start()

    def gather(s):
        if s < A:
            pl.when(z - s >= 0)(functools.partial(gather_from_left, s))
            pl.when(z + s < A)(functools.partial(gather_from_right, s))

    terms(order(0), y)
    give_y(order(A - 1))
    gather(1)
    for i in range(1, A):
        terms(order(i), y)
    for s in range(1, A):
        far = A - s
        gather(s + 1)
        pl.when(z + far < A)(functools.partial(send_sum_right, far))
        pl.when(z - far >= 0)(functools.partial(send_sum_left, far))

    out_ref[...] = summed(z)

    @pl.when(has_left)
    def _():
        arrived(z)
        out_ref[...] = out_ref[...] + rz[z].astype(F32)

    @pl.when(has_right)
    def _():
        arrived(A)
        out_ref[...] = out_ref[...] + rz[A].astype(F32)

    xs[...] = out_ref[...].astype(BF16)

    def visit(fn):
        fn(fy)
        for s in range(1, A):
            @pl.when(z - s >= 0)
            def _():
                fn((z - s) * 2)
                fn((z - s) * 2 + 1)

            @pl.when(z + s < A)
            def _():
                fn((z + s) * 2)
                fn((z + s) * 2 + 1)

    def relay(fb):
        ag_landed(fb, dx, axr.at[fb])
        ag_core(fb, 1).start()

    visit(relay)

    def finish(fb):
        ag_landed(fb, dc, acr.at[0, fb])
        ag_landed(fb, dxc, acr.at[1, fb])
        ag_x(fb).wait_send()
        ag_core(fb, 0).wait_send()
        ag_core(fb, 1).wait_send()

    visit(finish)

    keep.wait()
    own_y.wait_send()
    for fb in (f, fy):
        pl.when(has_left)(lambda: ag_left(fb, own).wait_send())
        pl.when(has_right)(lambda: ag_right(fb, own).wait_send())
    for b in range(A):
        to_core(b, 0).wait_send()
        to_core(b, 1).wait_send()
        to_y(b).wait_send()
    for s in range(1, A):
        @pl.when(z + s < A)
        def _():
            to_right(z + s).wait_send()
            for yy in range(2):
                pl.when(has_left)(lambda: ag_left((z + s) * 2 + yy, own).wait_send())

        @pl.when(z - s >= 0)
        def _():
            to_left(z - s).wait_send()
            for yy in range(2):
                pl.when(has_right)(lambda: ag_right((z - s) * 2 + yy, own).wait_send())


def apply_kernel(
    rows_ref, cols_ref, tok_ref, gain_ref, tiles_hbm, cot_hbm, proj_hbm, tgrad_ref, ggrad_ref,
    tiles_ref, cot_ref, proj_ref, normed, outsum, back, sems,
):
    number, tile = tiles_ref.shape[0], tiles_ref.shape[1]
    count, width = tok_ref.shape
    fetch_cot = pltpu.make_async_copy(cot_hbm, cot_ref, sems.at[0])
    fetch_tiles = pltpu.make_async_copy(tiles_hbm, tiles_ref, sems.at[1])
    store = pltpu.make_async_copy(proj_ref, proj_hbm, sems.at[2])
    fetch_cot.start()
    fetch_tiles.start()
    scale = row_scale(tok_ref, width, tile)
    for b in range(width // tile):
        at = slice(b * tile, (b + 1) * tile)
        normed[b] = (tok_ref[:, at].astype(F32) * scale * gain_ref[:, at]).astype(BF16)
        back[b] = jnp.zeros((count, tile), F32)

    def clear(b, carry):
        outsum[b] = jnp.zeros((count, tile), F32)
        return carry

    lax.fori_loop(0, outsum.shape[0], clear, 0)
    fetch_cot.wait()
    fetch_tiles.wait()

    def body(i, carry):
        forward, backward, places = [], [], []
        for u in range(UNROLL):
            k = i * UNROLL + u
            r, c = rows_ref[k], cols_ref[k]
            places.append((r, c))
            weight = tiles_ref[k]
            g = cot_ref[:, pl.ds(pl.multiple_of(c * tile, tile), tile)]
            forward.append(jnp.dot(normed[r], weight, preferred_element_type=F32))
            backward.append(lax.dot_general(g, weight, (((1,), (1,)), ((), ())), preferred_element_type=F32))
        for u in range(UNROLL):
            r, c = places[u]
            outsum[c] = outsum[c] + forward[u]
            back[r] = back[r] + backward[u]
        return carry

    lax.fori_loop(0, number // UNROLL, body, 0)

    for b in range(outsum.shape[0]):
        proj_ref[:, b * tile:(b + 1) * tile] = outsum[b].astype(BF16)
    store.start()
    inner = jnp.zeros((count, tile), F32)
    for b in range(width // tile):
        at = slice(b * tile, (b + 1) * tile)
        x = tok_ref[:, at].astype(F32)
        dn = back[b]
        inner = inner + x * gain_ref[:, at] * dn
        ggrad_ref[b:b + 1, :] = jnp.sum(dn * x * scale, axis=0, keepdims=True)
    inner = jnp.sum(inner, axis=-1, keepdims=True) / width
    weight = scale * scale * scale * inner
    for b in range(width // tile):
        at = slice(b * tile, (b + 1) * tile)
        x = tok_ref[:, at].astype(F32)
        tgrad_ref[:, at] = (scale * gain_ref[:, at] * back[b] - x * weight).astype(BF16)
    store.wait()


def finish_kernel(
    nf, nd, part_ref, xs, gain_out, out_ref, got_d, got_f, rx, send_d, recv_d, send_f, recv_f, xss, xrs, fs, fr,
):
    f, d = lax.axis_index("fsdp"), lax.axis_index("dp")
    x, c = d // 2, d % 2
    dc = x * 2 + (1 - c)
    dx = (1 - x) * 2 + c
    h = xs.shape[0]
    pieces = fs.shape[0]
    size = h // pieces
    barrier = pltpu.get_barrier_semaphore()
    for o in range(1, nd):
        pl.semaphore_signal(barrier, inc=1, device_id={"fsdp": f, "dp": (d + o) % nd}, device_id_type=MESH)
    for o in range(1, nf):
        pl.semaphore_signal(barrier, inc=1, device_id={"fsdp": (f + o) % nf, "dp": d}, device_id_type=MESH)
    got_d[d] = part_ref[...]
    pl.semaphore_wait(barrier, nd - 1 + nf - 1)

    def copies(n, me, got, send, recv, place):
        return [remote(got.at[me], got.at[me], send.at[o], recv.at[me], *place((me + o) % n)) for o in range(1, n)]

    def total(n, me, got, send, recv, place):
        for o in range(1, n):
            there = (me + o) % n
            remote(got.at[there], got.at[there], send.at[o], recv.at[there], *place(there)).wait_recv()
        result = got[0]
        for k in range(1, n):
            result = result + got[k]
        return result

    def across(p):
        at = pl.ds(p * size, size)
        return remote(xs.at[at], rx.at[at], xss.at[p], xrs.at[p], f, dx)

    def to_core(p, core):
        at = pl.ds(core * h + p * size, size)
        return remote(out_ref.at[at], out_ref.at[at], fs.at[p], fr.at[p], f, dc)

    replicas = (nd, d, got_d, send_d, recv_d, lambda dd: (f, dd))
    owners = (nf, f, got_f, send_f, recv_f, lambda ff: (ff, d))
    first = copies(*replicas)
    for copy in first:
        copy.start()
    for p in range(pieces):
        across(p).start()
    got_f[f] = total(*replicas)
    second = copies(*owners)
    for copy in second:
        copy.start()
    for p in range(pieces):
        across(p).wait_recv()
        at = pl.ds(p * size, size)
        out_ref[pl.ds(c * h + p * size, size)] = xs[at].astype(F32) + rx[at].astype(F32)
        to_core(p, c).start()
    gain_out[...] = total(*owners)
    for p in range(pieces):
        to_core(p, 1 - c).wait_recv()
    for copy in first + second:
        copy.wait_send()
    for p in range(pieces):
        across(p).wait_send()
        to_core(p, c).wait_send()


def solution(mesh):
    nf, nd = mesh.shape["fsdp"], mesh.shape["dp"]
    A = nf // 2
    vmem = pl.BlockSpec(memory_space=pltpu.VMEM)
    smem = pl.BlockSpec(memory_space=pltpu.SMEM)
    anywhere = pl.BlockSpec(memory_space=pl.ANY)
    dma = pltpu.SemaphoreType.DMA
    params = functools.partial(pltpu.CompilerParams, vmem_limit_bytes=60 * 2**20)

    def shards(tokens, gain, tiles, tile_rows, tile_cols, cotangent):
        count, width = tokens.shape
        group, tile, _ = tiles.shape
        number = group * nf
        rb, cb = width // tile, cotangent.shape[1] // tile
        h = group // 2
        gain2 = gain.reshape(1, width)

        gathered, summed = pl.pallas_call(
            functools.partial(comm_kernel, A),
            out_shape=(
                jax.ShapeDtypeStruct((nf, group, tile, tile), BF16),
                jax.ShapeDtypeStruct((h, tile, tile), BF16),
            ),
            in_specs=[smem, smem, vmem, vmem, anywhere, anywhere],
            out_specs=(anywhere, vmem),
            scratch_shapes=[
                pltpu.VMEM(cotangent.shape, BF16),
                pltpu.VMEM((h, tile, tile), F32),
                pltpu.VMEM((rb, tile, count), BF16),
                pltpu.VMEM((cb, count, tile), BF16),
                pltpu.VMEM((nf, group, tile, tile), BF16),
                pltpu.VMEM((nf, h, tile, tile), BF16),
                pltpu.VMEM((A, h, tile, tile), BF16),
                pltpu.VMEM((A + 1, h, tile, tile), BF16),
                dma, dma,
                dma((nf,)), dma((nf,)),
                dma((A,)), dma((A,)),
                dma((A,)), dma((A + 1,)),
                dma, dma,
                dma((2, nf)), dma((nf,)),
                dma((nf,)), dma((nf,)),
                dma((2, nf)), dma((2, nf)),
            ],
            compiler_params=params(collective_id=0, has_side_effects=True),
        )(tile_rows, tile_cols, tokens, gain2, cotangent, tiles)

        projected, token_grad, gain_part = pl.pallas_call(
            apply_kernel,
            out_shape=(
                jax.ShapeDtypeStruct(cotangent.shape, BF16),
                jax.ShapeDtypeStruct(tokens.shape, BF16),
                jax.ShapeDtypeStruct((rb, tile), F32),
            ),
            in_specs=[smem, smem, vmem, vmem, anywhere, anywhere],
            out_specs=(anywhere, vmem, vmem),
            scratch_shapes=[
                pltpu.VMEM((number, tile, tile), BF16),
                pltpu.VMEM(cotangent.shape, BF16),
                pltpu.VMEM(cotangent.shape, BF16),
                pltpu.VMEM((rb, count, tile), BF16),
                pltpu.VMEM((cb, count, tile), F32),
                pltpu.VMEM((rb, count, tile), F32),
                dma((3,)),
            ],
            compiler_params=params(),
        )(tile_rows, tile_cols, tokens, gain2, gathered.reshape(number, tile, tile), cotangent)

        pieces = 4 if h % 4 == 0 else 1
        gain_grad, tile_grad = pl.pallas_call(
            functools.partial(finish_kernel, nf, nd),
            out_shape=(
                jax.ShapeDtypeStruct((rb, tile), F32),
                jax.ShapeDtypeStruct((group, tile, tile), F32),
            ),
            in_specs=[vmem, vmem],
            out_specs=(vmem, vmem),
            scratch_shapes=[
                pltpu.VMEM((nd, rb, tile), F32),
                pltpu.VMEM((nf, rb, tile), F32),
                pltpu.VMEM((h, tile, tile), BF16),
                dma((nd,)), dma((nd,)), dma((nf,)), dma((nf,)),
                dma((pieces,)), dma((pieces,)), dma((pieces,)), dma((pieces,)),
            ],
            compiler_params=params(collective_id=1, has_side_effects=True),
        )(gain_part, summed)
        return (projected, token_grad, tile_grad, gain_grad.reshape(width))

    data = P(("fsdp", "dp"), None)
    return jax.shard_map(
        shards,
        mesh=mesh,
        in_specs=(data, P(), P("fsdp", None, None), P(), P(), data),
        out_specs=(data, data, P("fsdp", None, None), P()),
        check_vma=False,
    )
```

```python
import functools

import jax
import jax.numpy as jnp
from jax import lax
from jax.experimental import pallas as pl
from jax.experimental.pallas import tpu as pltpu
from jax.sharding import PartitionSpec as P

MESH = pl.DeviceIdType.MESH
F32 = jnp.float32
BF16 = jnp.bfloat16
UNROLL = 8


def remote(src, dst, send, recv, f, d):
    return pltpu.make_async_remote_copy(
        src_ref=src, dst_ref=dst, send_sem=send, recv_sem=recv,
        device_id={"fsdp": f, "dp": d}, device_id_type=MESH,
    )


def row_scale(tok_ref, width, tile):
    total = jnp.zeros((tok_ref.shape[0], tile), F32)
    for b in range(width // tile):
        x = tok_ref[:, b * tile:(b + 1) * tile].astype(F32)
        total = total + x * x
    mean = jnp.sum(total, axis=-1, keepdims=True) / width
    return lax.rsqrt(mean + 1e-05)


def comm_kernel(
    A, rows_ref, cols_ref, tok_ref, gain_ref, cot_hbm, tiles_ref, ag, xs,
    cot_ref, out_ref, normed_t, cot_blocks, part_ref, rc, ry, rz,
    csem, lsem, cs, cr, ys, yr, zs, zr,
    ays, ayr, azs, azr, axs, axr, acs, acr,
):
    f, d = lax.axis_index("fsdp"), lax.axis_index("dp")
    z, y = f // 2, f % 2
    x, c = d // 2, d % 2
    fy = z * 2 + (1 - y)
    dc = x * 2 + (1 - c)
    dx = (1 - x) * 2 + c
    dxc = (1 - x) * 2 + (1 - c)
    group = tiles_ref.shape[0]
    h, q = group // 2, group // 4
    tile, width = tiles_ref.shape[1], tok_ref.shape[1]
    has_left, has_right = z > 0, z < A - 1
    fetch = pltpu.make_async_copy(cot_hbm, cot_ref, csem)
    fetch.start()

    barrier = pltpu.get_barrier_semaphore()

    def greet(ff, dd):
        pl.semaphore_signal(barrier, inc=1, device_id={"fsdp": ff, "dp": dd}, device_id_type=MESH)

    greet(f, dc)
    greet(f, dx)
    greet(fy, d)
    pl.when(has_left)(lambda: greet(f - 2, d))
    pl.when(has_right)(lambda: greet(f + 2, d))
    pl.semaphore_wait(barrier, 3 + has_left.astype(jnp.int32) + has_right.astype(jnp.int32))

    def quarter(fb, dd):
        return ag.at[fb, pl.ds(dd * q, q)]

    def to_core(b, yy):
        fb = b * 2 + yy
        return remote(part_ref.at[fb, pl.ds((1 - c) * h, h)], rc.at[fb], cs.at[fb], cr.at[fb], f, dc)

    def to_y(b):
        return remote(rc.at[b * 2 + 1 - y], ry.at[b], ys.at[b], yr.at[b], fy, d)

    def to_right(b):
        return remote(rc.at[b * 2 + y], rz.at[b], zs.at[b], zr.at[b], f + 2, d)

    def to_left(b):
        slot = jnp.where(b == z - 1, A, b)
        return remote(rc.at[b * 2 + y], rz.at[slot], zs.at[b], zr.at[slot], f - 2, d)

    def arrived(slot):
        remote(rz.at[slot], rz.at[slot], zs.at[0], zr.at[slot], fy, d).wait_recv()

    own = tiles_ref.at[pl.ds(d * q, q)]
    own_y = remote(own, quarter(f, d), ays, ayr, fy, d)

    def ag_left(fb, src):
        return remote(src, quarter(fb, d), azs.at[0, fb], azr.at[fb], f - 2, d)

    def ag_right(fb, src):
        return remote(src, quarter(fb, d), azs.at[1, fb], azr.at[fb], f + 2, d)

    def ag_x(fb):
        return remote(quarter(fb, d), quarter(fb, d), axs.at[fb], axr.at[fb], f, dx)

    def ag_core(fb, which):
        dd = d if which == 0 else dx
        return remote(quarter(fb, dd), quarter(fb, dd), acs.at[which, fb], acr.at[which, fb], f, dc)

    def ag_landed(fb, dd, sem):
        remote(quarter(fb, dd), quarter(fb, dd), ays, sem, fy, d).wait_recv()

    def spread(fb):
        ag_x(fb).start()
        ag_core(fb, 0).start()

    own_y.start()
    pl.when(has_left)(lambda: ag_left(f, own).start())
    pl.when(has_right)(lambda: ag_right(f, own).start())
    keep = pltpu.make_async_copy(tiles_ref, ag.at[f], lsem)
    keep.start()

    after, before = A - 1 - z, z
    more_after = after >= before
    alone = jnp.where(more_after, after - before, before - after)
    paired = jnp.where(more_after, before, after)

    def order(i):
        j = i - alone
        step = paired - j // 2
        pair = jnp.where(j % 2 == 0, z + step, z - step)
        return jnp.where(i < alone, jnp.where(more_after, A - 1 - i, i), pair)

    scale = row_scale(tok_ref, width, tile)
    for b in range(width // tile):
        at = slice(b * tile, (b + 1) * tile)
        normed_t[b] = (tok_ref[:, at].astype(F32) * scale * gain_ref[:, at]).T.astype(BF16)

    fetch.wait()
    for b in range(cot_ref.shape[1] // tile):
        cot_blocks[b] = cot_ref[:, b * tile:(b + 1) * tile]

    def terms(b, yy):
        fb = b * 2 + yy

        def body(i, carry):
            found = []
            for u in range(UNROLL):
                k = fb * group + i * UNROLL + u
                found.append(jnp.dot(normed_t[rows_ref[k]], cot_blocks[cols_ref[k]], preferred_element_type=F32))
            for u in range(UNROLL):
                part_ref[fb, i * UNROLL + u] = found[u].astype(BF16)
            return carry

        lax.fori_loop(0, group // UNROLL, body, 0)
        to_core(b, yy).start()

    def halves(fb):
        return part_ref[fb, pl.ds(c * h, h)].astype(F32) + rc[fb].astype(F32)

    def give_y(b):
        fb = b * 2 + 1 - y
        to_core(b, 1 - y).wait_recv()
        rc[fb] = halves(fb).astype(BF16)
        to_y(b).start()

    for i in range(A):
        terms(order(i), 1 - y)
        if i == 0:
            ag_landed(fy, d, ayr)
            pl.when(has_left)(lambda: ag_left(fy, quarter(fy, d)).start())
            pl.when(has_right)(lambda: ag_right(fy, quarter(fy, d)).start())
            spread(fy)
        else:
            give_y(order(i - 1))

    def summed(b):
        to_core(b, y).wait_recv()
        to_y(b).wait_recv()
        return halves(b * 2 + y) + ry[b].astype(F32)

    def gather_from_left(s):
        b = z - s
        for yy in range(2):
            fb = b * 2 + yy
            ag_landed(fb, d, azr.at[fb])
            pl.when(has_right)(lambda: ag_right(fb, quarter(fb, d)).start())
            spread(fb)

    def gather_from_right(s):
        b = z + s
        for yy in range(2):
            fb = b * 2 + yy
            ag_landed(fb, d, azr.at[fb])
            pl.when(has_left)(lambda: ag_left(fb, quarter(fb, d)).start())
            spread(fb)

    def send_sum_right(s):
        b = z + s
        fb = b * 2 + y
        rc[fb] = summed(b).astype(BF16)

        @pl.when(has_left)
        def _():
            arrived(b)
            rc[fb] = (rc[fb].astype(F32) + rz[b].astype(F32)).astype(BF16)

        to_right(b).start()

    def send_sum_left(s):
        b = z - s
        fb = b * 2 + y
        rc[fb] = summed(b).astype(BF16)

        @pl.when(has_right)
        def _():
            arrived(b)
            rc[fb] = (rc[fb].astype(F32) + rz[b].astype(F32)).astype(BF16)

        to_left(b).start()

    def gather(s):
        if s < A:
            pl.when(z - s >= 0)(functools.partial(gather_from_left, s))
            pl.when(z + s < A)(functools.partial(gather_from_right, s))

    terms(order(0), y)
    give_y(order(A - 1))
    gather(1)
    for i in range(1, A):
        terms(order(i), y)
    for s in range(1, A):
        far = A - s
        gather(s + 1)
        pl.when(z + far < A)(functools.partial(send_sum_right, far))
        pl.when(z - far >= 0)(functools.partial(send_sum_left, far))

    out_ref[...] = summed(z)

    @pl.when(has_left)
    def _():
        arrived(z)
        out_ref[...] = out_ref[...] + rz[z].astype(F32)

    @pl.when(has_right)
    def _():
        arrived(A)
        out_ref[...] = out_ref[...] + rz[A].astype(F32)

    xs[...] = out_ref[...].astype(BF16)

    def visit(fn):
        fn(fy)
        for s in range(1, A):
            @pl.when(z - s >= 0)
            def _():
                fn((z - s) * 2)
                fn((z - s) * 2 + 1)

            @pl.when(z + s < A)
            def _():
                fn((z + s) * 2)
                fn((z + s) * 2 + 1)

    def relay(fb):
        ag_landed(fb, dx, axr.at[fb])
        ag_core(fb, 1).start()

    visit(relay)

    def finish(fb):
        ag_landed(fb, dc, acr.at[0, fb])
        ag_landed(fb, dxc, acr.at[1, fb])
        ag_x(fb).wait_send()
        ag_core(fb, 0).wait_send()
        ag_core(fb, 1).wait_send()

    visit(finish)

    keep.wait()
    own_y.wait_send()
    for fb in (f, fy):
        pl.when(has_left)(lambda: ag_left(fb, own).wait_send())
        pl.when(has_right)(lambda: ag_right(fb, own).wait_send())
    for b in range(A):
        to_core(b, 0).wait_send()
        to_core(b, 1).wait_send()
        to_y(b).wait_send()
    for s in range(1, A):
        @pl.when(z + s < A)
        def _():
            to_right(z + s).wait_send()
            for yy in range(2):
                pl.when(has_left)(lambda: ag_left((z + s) * 2 + yy, own).wait_send())

        @pl.when(z - s >= 0)
        def _():
            to_left(z - s).wait_send()
            for yy in range(2):
                pl.when(has_right)(lambda: ag_right((z - s) * 2 + yy, own).wait_send())


def apply_kernel(
    rows_ref, cols_ref, tok_ref, gain_ref, tiles_hbm, cot_hbm, proj_hbm, tgrad_ref, ggrad_ref,
    tiles_ref, cot_ref, proj_ref, normed, outsum, back, sems,
):
    number, tile = tiles_ref.shape[0], tiles_ref.shape[1]
    count, width = tok_ref.shape
    fetch_cot = pltpu.make_async_copy(cot_hbm, cot_ref, sems.at[0])
    fetch_tiles = pltpu.make_async_copy(tiles_hbm, tiles_ref, sems.at[1])
    store = pltpu.make_async_copy(proj_ref, proj_hbm, sems.at[2])
    fetch_cot.start()
    fetch_tiles.start()
    scale = row_scale(tok_ref, width, tile)
    for b in range(width // tile):
        at = slice(b * tile, (b + 1) * tile)
        normed[b] = (tok_ref[:, at].astype(F32) * scale * gain_ref[:, at]).astype(BF16)
        back[b] = jnp.zeros((count, tile), F32)

    def clear(b, carry):
        outsum[b] = jnp.zeros((count, tile), F32)
        return carry

    lax.fori_loop(0, outsum.shape[0], clear, 0)
    fetch_cot.wait()
    fetch_tiles.wait()

    def body(i, carry):
        forward, backward, places = [], [], []
        for u in range(UNROLL):
            k = i * UNROLL + u
            r, c = rows_ref[k], cols_ref[k]
            places.append((r, c))
            weight = tiles_ref[k]
            g = cot_ref[:, pl.ds(pl.multiple_of(c * tile, tile), tile)]
            forward.append(jnp.dot(normed[r], weight, preferred_element_type=F32))
            backward.append(lax.dot_general(g, weight, (((1,), (1,)), ((), ())), preferred_element_type=F32))
        for u in range(UNROLL):
            r, c = places[u]
            outsum[c] = outsum[c] + forward[u]
            back[r] = back[r] + backward[u]
        return carry

    lax.fori_loop(0, number // UNROLL, body, 0)

    for b in range(outsum.shape[0]):
        proj_ref[:, b * tile:(b + 1) * tile] = outsum[b].astype(BF16)
    store.start()
    inner = jnp.zeros((count, tile), F32)
    for b in range(width // tile):
        at = slice(b * tile, (b + 1) * tile)
        x = tok_ref[:, at].astype(F32)
        dn = back[b]
        inner = inner + x * gain_ref[:, at] * dn
        ggrad_ref[b:b + 1, :] = jnp.sum(dn * x * scale, axis=0, keepdims=True)
    inner = jnp.sum(inner, axis=-1, keepdims=True) / width
    weight = scale * scale * scale * inner
    for b in range(width // tile):
        at = slice(b * tile, (b + 1) * tile)
        x = tok_ref[:, at].astype(F32)
        tgrad_ref[:, at] = (scale * gain_ref[:, at] * back[b] - x * weight).astype(BF16)
    store.wait()


def finish_kernel(
    nf, nd, part_ref, xs, gain_out, near, far, got_d, got_f, send_d, recv_d, send_f, recv_f, xss, xrs, ns, nr, fs, fr,
):
    f, d = lax.axis_index("fsdp"), lax.axis_index("dp")
    x, c = d // 2, d % 2
    dc = x * 2 + (1 - c)
    dx = (1 - x) * 2 + c
    h = xs.shape[0]
    pieces = fs.shape[0]
    size = h // pieces
    barrier = pltpu.get_barrier_semaphore()
    for o in range(1, nd):
        pl.semaphore_signal(barrier, inc=1, device_id={"fsdp": f, "dp": (d + o) % nd}, device_id_type=MESH)
    for o in range(1, nf):
        pl.semaphore_signal(barrier, inc=1, device_id={"fsdp": (f + o) % nf, "dp": d}, device_id_type=MESH)
    got_d[d] = part_ref[...]
    pl.semaphore_wait(barrier, nd - 1 + nf - 1)

    def copies(n, me, got, send, recv, place):
        return [remote(got.at[me], got.at[me], send.at[o], recv.at[me], *place((me + o) % n)) for o in range(1, n)]

    def total(n, me, got, send, recv, place):
        for o in range(1, n):
            there = (me + o) % n
            remote(got.at[there], got.at[there], send.at[o], recv.at[there], *place(there)).wait_recv()
        result = got[0]
        for k in range(1, n):
            result = result + got[k]
        return result

    def across(p):
        at = pl.ds(p * size, size)
        return remote(xs.at[at], far.at[pl.ds(c * h + p * size, size)], xss.at[p], xrs.at[p], f, dx)

    def near_core(core):
        return remote(xs, near.at[pl.ds(core * h, h)], ns, nr, f, dc)

    def to_core(p, core):
        at = pl.ds(core * h + p * size, size)
        return remote(far.at[at], far.at[at], fs.at[p], fr.at[p], f, dc)

    replicas = (nd, d, got_d, send_d, recv_d, lambda dd: (f, dd))
    owners = (nf, f, got_f, send_f, recv_f, lambda ff: (ff, d))
    first = copies(*replicas)
    for copy in first:
        copy.start()
    for p in range(pieces):
        across(p).start()
    near_core(c).start()
    near[pl.ds(c * h, h)] = xs[...]
    got_f[f] = total(*replicas)
    second = copies(*owners)
    for copy in second:
        copy.start()
    for p in range(pieces):
        across(p).wait_recv()
        to_core(p, c).start()
    gain_out[...] = total(*owners)
    near_core(1 - c).wait_recv()
    for p in range(pieces):
        to_core(p, 1 - c).wait_recv()
    near_core(c).wait_send()
    for copy in first + second:
        copy.wait_send()
    for p in range(pieces):
        across(p).wait_send()
        to_core(p, c).wait_send()


def solution(mesh):
    nf, nd = mesh.shape["fsdp"], mesh.shape["dp"]
    A = nf // 2
    vmem = pl.BlockSpec(memory_space=pltpu.VMEM)
    smem = pl.BlockSpec(memory_space=pltpu.SMEM)
    anywhere = pl.BlockSpec(memory_space=pl.ANY)
    dma = pltpu.SemaphoreType.DMA
    params = functools.partial(pltpu.CompilerParams, vmem_limit_bytes=60 * 2**20)

    def shards(tokens, gain, tiles, tile_rows, tile_cols, cotangent):
        count, width = tokens.shape
        group, tile, _ = tiles.shape
        number = group * nf
        rb, cb = width // tile, cotangent.shape[1] // tile
        h = group // 2
        gain2 = gain.reshape(1, width)

        gathered, summed = pl.pallas_call(
            functools.partial(comm_kernel, A),
            out_shape=(
                jax.ShapeDtypeStruct((nf, group, tile, tile), BF16),
                jax.ShapeDtypeStruct((h, tile, tile), BF16),
            ),
            in_specs=[smem, smem, vmem, vmem, anywhere, anywhere],
            out_specs=(anywhere, vmem),
            scratch_shapes=[
                pltpu.VMEM(cotangent.shape, BF16),
                pltpu.VMEM((h, tile, tile), F32),
                pltpu.VMEM((rb, tile, count), BF16),
                pltpu.VMEM((cb, count, tile), BF16),
                pltpu.VMEM((nf, group, tile, tile), BF16),
                pltpu.VMEM((nf, h, tile, tile), BF16),
                pltpu.VMEM((A, h, tile, tile), BF16),
                pltpu.VMEM((A + 1, h, tile, tile), BF16),
                dma, dma,
                dma((nf,)), dma((nf,)),
                dma((A,)), dma((A,)),
                dma((A,)), dma((A + 1,)),
                dma, dma,
                dma((2, nf)), dma((nf,)),
                dma((nf,)), dma((nf,)),
                dma((2, nf)), dma((2, nf)),
            ],
            compiler_params=params(collective_id=0, has_side_effects=True),
        )(tile_rows, tile_cols, tokens, gain2, cotangent, tiles)

        projected, token_grad, gain_part = pl.pallas_call(
            apply_kernel,
            out_shape=(
                jax.ShapeDtypeStruct(cotangent.shape, BF16),
                jax.ShapeDtypeStruct(tokens.shape, BF16),
                jax.ShapeDtypeStruct((rb, tile), F32),
            ),
            in_specs=[smem, smem, vmem, vmem, anywhere, anywhere],
            out_specs=(anywhere, vmem, vmem),
            scratch_shapes=[
                pltpu.VMEM((number, tile, tile), BF16),
                pltpu.VMEM(cotangent.shape, BF16),
                pltpu.VMEM(cotangent.shape, BF16),
                pltpu.VMEM((rb, count, tile), BF16),
                pltpu.VMEM((cb, count, tile), F32),
                pltpu.VMEM((rb, count, tile), F32),
                dma((3,)),
            ],
            compiler_params=params(),
        )(tile_rows, tile_cols, tokens, gain2, gathered.reshape(number, tile, tile), cotangent)

        pieces = 4 if h % 4 == 0 else 1
        gain_grad, near, far = pl.pallas_call(
            functools.partial(finish_kernel, nf, nd),
            out_shape=(
                jax.ShapeDtypeStruct((rb, tile), F32),
                jax.ShapeDtypeStruct((group, tile, tile), BF16),
                jax.ShapeDtypeStruct((group, tile, tile), BF16),
            ),
            in_specs=[vmem, vmem],
            out_specs=(vmem, vmem, vmem),
            scratch_shapes=[
                pltpu.VMEM((nd, rb, tile), F32),
                pltpu.VMEM((nf, rb, tile), F32),
                dma((nd,)), dma((nd,)), dma((nf,)), dma((nf,)),
                dma((pieces,)), dma((pieces,)), dma, dma, dma((pieces,)), dma((pieces,)),
            ],
            compiler_params=params(collective_id=1, has_side_effects=True),
        )(gain_part, summed)
        tile_grad = near.astype(F32) + far.astype(F32)
        return (projected, token_grad, tile_grad, gain_grad.reshape(width))

    data = P(("fsdp", "dp"), None)
    return jax.shard_map(
        shards,
        mesh=mesh,
        in_specs=(data, P(), P("fsdp", None, None), P(), P(), data),
        out_specs=(data, data, P("fsdp", None, None), P()),
        check_vma=False,
    )
```
